768 devices in a mesh: dp: 16 (over y, core), expert: 48 (over z, x).
Axes of the slice: x: 4, y: 8, z: 12, core: 2. Of those that a mesh axis runs over, the one named last changes fastest.
Arguments:
- d_out: bfloat16 [7680, 3072], P(('dp', 'expert')), may hold values from -6 to 6
- routes: int32 [7680, 2], P(('dp', 'expert')), may hold values from 0 to 7, as said below
- probs: float32 [7680, 2], P(('dp', 'expert')), may hold values from 0.1 to 1
- saved_inputs: bfloat16 [16, 48, 240, 3072], P('dp', 'expert'), may hold values from -6 to 6
- w_gate: bfloat16 [18432, 3072], P('expert'), may hold values from -0.109375 to 0.109375
- w_up: bfloat16 [18432, 3072], P('expert'), may hold values from -0.109375 to 0.109375
- w_down: bfloat16 [18432, 3072], P('expert'), may hold values from -0.0625 to 0.0625
Outputs:
- input_grad: bfloat16 [7680, 3072], P(('dp', 'expert'))
- weight_grads: bfloat16 [3, 3072, 18432], P(None, 'dp', 'expert')
The draws below stay inside these ranges and needn't reach their ends.
Inputs may be any that keep to these rules, and one draw needn't show every extreme that they name: `routes`: the two experts of a token differ. Among the 10 rows of one device each expert below 2 is named at most 5 times, and one of them exactly 5 times.
All inputs are finite; a program needn't handle non-finite values.
Results may differ from the reference program's by a relative error of at most 0.023.
Values may be sent and summed in bfloat16 or wider, within the bound.
No kernel may reach another device: no remote copies, remote signals or barrier semaphores. Data moves between devices by JAX's collectives and lax.ppermute only.
A program may use at most 64 MiB of HBM per device.

```python
import jax
import jax.numpy as jnp
from jax import lax

D = 3072
EXPERTS = 2
HID = 9216
TOK_DEV = 10
CAP = 5
HID_DEV = 384
TOKENS = 7680
N_DP = 16
N_EXPERT = 48


def draw_routes(key, part):
    key = jax.random.fold_in(key, 11)
    blocks = TOKENS // TOK_DEV
    keys = jax.random.split(key, 7)
    rank = jax.vmap(lambda one: jax.random.permutation(one, TOK_DEV))(jax.random.split(keys[0], blocks)).astype(jnp.int32)
    full_expert = jax.random.randint(keys[1], (blocks, 1), 0, 2).astype(jnp.int32)
    other_count = jax.random.randint(keys[2], (blocks, 1), 1, CAP + 1).astype(jnp.int32)
    offset = jax.random.randint(keys[3], (blocks, 1), 0, TOK_DEV - other_count + 1).astype(jnp.int32)
    has_full = rank < CAP
    has_other = (rank >= offset) & (rank < offset + other_count)
    first_pick = jax.random.randint(keys[4], (blocks, TOK_DEV), 0, 6).astype(jnp.int32)
    second_pick = (first_pick + jax.random.randint(keys[5], (blocks, TOK_DEV), 1, 6).astype(jnp.int32)) % 6
    first_pick = first_pick + 2
    second_pick = second_pick + 2
    other_expert = 1 - full_expert
    first = jnp.where(has_full, full_expert, jnp.where(has_other, other_expert, first_pick))
    second = jnp.where(has_full, jnp.where(has_other, other_expert, first_pick), jnp.where(has_other, first_pick, second_pick))
    flip = jax.random.randint(keys[6], (blocks, TOK_DEV), 0, 2).astype(jnp.int32)
    column_one = jnp.where(flip == 1, second, first)
    column_two = jnp.where(flip == 1, first, second)
    return jnp.stack([column_one, column_two], axis=-1).reshape(TOKENS, 2).astype(jnp.int32)


def strengthened(values, own_key, source, target, parts, factor):
    owner, partner = [(jnp.arange(values.shape[axis_at]) // (values.shape[axis_at] // parts)).reshape([-1 if axis == axis_at else 1 for axis in range(values.ndim)]) for axis_at in (source, target)]
    chosen = jax.random.permutation(own_key, parts)[partner]
    strong = (owner == chosen) | (owner == (partner + parts // 2) % parts)
    return jnp.where(strong, factor * values, values)


def block_levels(key, shape, shards, least, largest):
    def one(dim, blocks):
        heights = jax.random.uniform(jax.random.fold_in(jax.random.fold_in(key, 6), dim), (blocks,), jnp.float32, least / len(shards), largest / len(shards))
        return jnp.repeat(jnp.exp(heights), shape[dim] // blocks).reshape((-1,) + (1,) * (len(shape) - dim - 1))

    loudness = one(*shards[0])
    for cut in shards[1:]:
        loudness = loudness * one(*cut)
    return loudness


def scatter_about(rng, dims, scale, reach, shards=(), kind=jnp.bfloat16):
    level = block_levels(rng, dims, shards, -0.22, 0.18) if shards else 1.0
    entries = jax.random.normal(rng, dims, jnp.float32) * scale * level
    return jnp.minimum(jnp.maximum(entries, -reach), reach).astype(kind)


def gaussian_with(rng, shape, spread, limit, shards, heavy, kind=jnp.bfloat16):
    result = spread * jax.random.normal(rng, shape, jnp.float32)
    if shards:
        result = result * block_levels(rng, shape, shards, -0.22, 0.18)
    return jnp.clip(strengthened(result, jax.random.fold_in(rng, 3), *heavy), -limit, limit).astype(kind)


def setup_inputs(seed: int = 0) -> dict:
    key_list = jax.random.split(jax.random.key(seed), 8)
    d_out = scatter_about(key_list[0], (TOKENS, D), 1.0, 6.0, ((0, 768),))
    routes = draw_routes(jax.random.fold_in(key_list[7], 71), 0)
    probs = jnp.clip(0.1 + 0.9 * jax.random.uniform(key_list[2], (TOKENS, 2), jnp.float32) ** block_levels(key_list[2], (TOKENS, 2), ((0, 768),), -0.2, 0.2), 0.1, 1.0)
    saved_inputs = gaussian_with(key_list[3], (N_DP, N_EXPERT, N_EXPERT * CAP, D), 1.0, 6.0, ((0, 16), (1, 48)), (0, 3, 16, 2.0))
    w_gate = scatter_about(key_list[4], (EXPERTS * HID, D), D ** -0.5, 0.109375, ((0, 48),))
    w_up = scatter_about(key_list[5], (EXPERTS * HID, D), D ** -0.5, 0.109375, ((0, 48),))
    w_down = scatter_about(key_list[6], (EXPERTS * HID, D), HID ** -0.5, 0.0625, ((0, 48),))
    return dict(d_out=d_out, routes=routes, probs=probs, saved_inputs=saved_inputs, w_gate=w_gate, w_up=w_up, w_down=w_down)


def slot_table(routes_dev):
    flat = routes_dev.reshape(-1).astype(jnp.int32)
    onehot = (flat[:, None] == jnp.arange(EXPERTS, dtype=jnp.int32)[None, :]).astype(jnp.int32)
    before = jnp.cumsum(onehot, axis=0) - onehot
    position = jnp.sum(before * onehot, axis=1).astype(jnp.int32)
    inside = flat < EXPERTS
    return jnp.where(inside, flat * CAP + position, EXPERTS * CAP).astype(jnp.int32)


def dispatch_rows(d_dev, routes_dev, probs_dev):
    index = slot_table(routes_dev)
    scaled = (probs_dev[:, :, None] * d_dev[:, None, :].astype(jnp.float32)).astype(jnp.bfloat16)
    scaled = scaled.reshape(-1, D)
    return jnp.zeros((EXPERTS * CAP, D), jnp.bfloat16).at[index].set(scaled, mode="drop")


def expert_work(rows_x, rows_dy, gate_block, up_block, down_block):
    contract = (((1,), (1,)), ((), ()))
    across = (((0,), (0,)), ((), ()))
    gate = lax.dot_general(rows_x, gate_block, contract, preferred_element_type=jnp.float32)
    upper = lax.dot_general(rows_x, up_block, contract, preferred_element_type=jnp.float32)
    sigma = jax.nn.sigmoid(gate)
    act = gate * sigma
    hidden = (act * upper).astype(jnp.bfloat16)
    d_hidden = lax.dot_general(rows_dy, down_block, contract, preferred_element_type=jnp.float32)
    d_up = (d_hidden * act).astype(jnp.bfloat16)
    d_gate = (d_hidden * upper * sigma * (1.0 + gate * (1.0 - sigma))).astype(jnp.bfloat16)
    partial_dx = (jnp.dot(d_gate, gate_block, preferred_element_type=jnp.float32)
                  + jnp.dot(d_up, up_block, preferred_element_type=jnp.float32)).astype(jnp.bfloat16)
    term_gate = lax.dot_general(rows_x, d_gate, across, preferred_element_type=jnp.float32)
    term_up = lax.dot_general(rows_x, d_up, across, preferred_element_type=jnp.float32)
    term_down = lax.dot_general(rows_dy, hidden, across, preferred_element_type=jnp.float32)
    terms = jnp.stack([term_gate, term_up, term_down], axis=0).astype(jnp.bfloat16)
    return partial_dx, terms


def reference(d_out, routes, probs, saved_inputs, w_gate, w_up, w_down):
    slices = N_EXPERT // EXPERTS
    d_dev = d_out.reshape(N_DP, N_EXPERT, TOK_DEV, D)
    r_dev = routes.reshape(N_DP, N_EXPERT, TOK_DEV, 2)
    p_dev = probs.reshape(N_DP, N_EXPERT, TOK_DEV, 2)
    gate_blocks = w_gate.reshape(N_EXPERT, HID_DEV, D)
    up_blocks = w_up.reshape(N_EXPERT, HID_DEV, D)
    down_blocks = w_down.reshape(N_EXPERT, HID_DEV, D)
    owners = jnp.arange(N_EXPERT, dtype=jnp.int32)

    def one_group(total, inputs):
        d_grp, r_grp, p_grp, x_grp = inputs
        sent = jax.vmap(dispatch_rows)(d_grp, r_grp, p_grp).reshape(N_EXPERT, EXPERTS, CAP, D)

        def one_owner(args):
            owner, rows_x, gate_block, up_block, down_block = args
            rows_dy = jnp.take(sent, owner // slices, axis=1).reshape(N_EXPERT * CAP, D)
            return expert_work(rows_x, rows_dy, gate_block, up_block, down_block)

        partial_dx, terms = lax.map(one_owner, (owners, x_grp, gate_blocks, up_blocks, down_blocks))
        partial_dx = partial_dx.reshape(N_EXPERT, N_EXPERT, CAP, D)

        def one_sender(args):
            sender, r_one = args
            back = jnp.take(partial_dx, sender, axis=1).astype(jnp.float32)
            summed = jnp.sum(back.reshape(EXPERTS, slices, CAP, D), axis=1).reshape(EXPERTS * CAP, D)
            index = slot_table(r_one)
            inside = (index < EXPERTS * CAP).astype(jnp.float32)
            picked = jnp.take(summed, jnp.minimum(index, EXPERTS * CAP - 1), axis=0) * inside[:, None]
            return jnp.sum(picked.reshape(TOK_DEV, 2, D), axis=1).astype(jnp.bfloat16)

        grads_in = lax.map(one_sender, (owners, r_grp))
        return total + terms.astype(jnp.float32), grads_in

    start = jnp.zeros((N_EXPERT, 3, D, HID_DEV), jnp.float32)
    total, grads_in = lax.scan(one_group, start, (d_dev, r_dev, p_dev, saved_inputs))
    weight_grads = total.astype(jnp.bfloat16).transpose(1, 2, 0, 3).reshape(3, D, N_EXPERT * HID_DEV)
    input_grad = grads_in.reshape(TOKENS, D)
    return input_grad, weight_grads
```

```python
import functools

import jax
import jax.numpy as jnp
from jax import lax
from jax.experimental import pallas as pl
from jax.experimental.pallas import tpu as pltpu
from jax.sharding import Mesh, PartitionSpec as P

EXPERTS = 2
SLOT_ROWS = 16
PARTS = 3
TILE = 256
F32 = jnp.float32
BF16 = jnp.bfloat16
LIMIT = 56 * 1024 * 1024
NT = (((1,), (1,)), ((), ()))
TN = (((0,), (0,)), ((), ()))
VMEM = pl.BlockSpec(memory_space=pltpu.VMEM)
SMEM = pl.BlockSpec(memory_space=pltpu.SMEM)


def call(body, out_shape, in_specs, scratch=(), flops=0, moved=0, **more):
    return pl.pallas_call(
        body,
        out_shape=out_shape,
        in_specs=in_specs,
        scratch_shapes=list(scratch),
        compiler_params=pltpu.CompilerParams(vmem_limit_bytes=LIMIT),
        cost_estimate=pl.CostEstimate(flops=flops, bytes_accessed=moved, transcendentals=0),
        **more,
    )


def walk(routes_ref, tokens):
    counts = [jnp.int32(0)] * EXPERTS
    for token in range(tokens):
        for choice in range(2):
            expert = routes_ref[choice, token]
            row = jnp.int32(EXPERTS * SLOT_ROWS)
            for e in range(EXPERTS):
                here = expert == e
                row = jnp.where(here, e * SLOT_ROWS + counts[e], row)
                counts[e] = counts[e] + here.astype(jnp.int32)
            yield token, choice, row


def pack_body(cap, routes_ref, probs_ref, d_ref, out_ref, rows):
    tokens, width = d_ref.shape
    part = width // PARTS
    rows[...] = jnp.zeros_like(rows)
    d = d_ref[...].astype(F32)
    for token, choice, row in walk(routes_ref, tokens):
        scaled = probs_ref[choice, token] * d[token : token + 1, :]
        for p in range(PARTS):
            rows[pl.ds(row + p * cap, 1), :] = scaled[:, p * part : (p + 1) * part]
    depth = out_ref.shape[0] // EXPERTS
    for e in range(EXPERTS):
        block = rows[e * SLOT_ROWS : (e + 1) * SLOT_ROWS, :].astype(BF16)
        for k in range(depth):
            out_ref[e * depth + k] = block


def eye():
    i = lax.broadcasted_iota(jnp.int32, (TILE, TILE), 0)
    j = lax.broadcasted_iota(jnp.int32, (TILE, TILE), 1)
    return (i == j).astype(BF16)


def split_halves(full, core, own_ref, other_ref, own):
    groups = full.shape[0] // (2 * own)
    for g in range(groups):
        mine = pl.multiple_of(g * 2 * own + core * own, 16)
        theirs = pl.multiple_of(g * 2 * own + (1 - core) * own, 16)
        own_ref[g * own : (g + 1) * own, :] = full[pl.ds(mine, own), :]
        other_ref[g * own : (g + 1) * own, :] = full[pl.ds(theirs, own), :]


def early_body(cap, n_x, block, own, where_ref, x_ref, wg_ref, wu_ref, own_ref, other_ref, act_ref, slope_ref, hidden_ref, xp, xt):
    rows, width = xp.shape
    used = x_ref.shape[0] // n_x
    at = where_ref[0]
    core = where_ref[1]
    r = lax.broadcasted_iota(jnp.int32, (rows, x_ref.shape[0]), 0)
    q = lax.broadcasted_iota(jnp.int32, (rows, x_ref.shape[0]), 1)
    i = r % block
    source = (at + r // block) % n_x
    order = ((q == ((i // cap) * n_x + source) * cap + i % cap) & (i < used)).astype(BF16)
    one = eye()
    for t in range(width // TILE):
        piece = jnp.dot(order, x_ref[:, t * TILE : (t + 1) * TILE], preferred_element_type=F32).astype(BF16)
        xp[:, t * TILE : (t + 1) * TILE] = piece
        xt[t * TILE : (t + 1) * TILE, :] = lax.dot_general(one, piece, NT, preferred_element_type=F32).astype(BF16)
    split_halves(xt, core, own_ref, other_ref, own)
    gate = lax.dot_general(xp[...], wg_ref[...], NT, preferred_element_type=F32)
    upper = lax.dot_general(xp[...], wu_ref[...], NT, preferred_element_type=F32)
    sigma = jax.nn.sigmoid(gate)
    act = gate * sigma
    act_ref[...] = act
    slope_ref[...] = upper * sigma * (1.0 + gate * (1.0 - sigma))
    hidden_ref[...] = (act * upper).astype(BF16)


def picker(cap, block, used, packed, part):
    i = lax.broadcasted_iota(jnp.int32, (block, packed), 0)
    q = lax.broadcasted_iota(jnp.int32, (block, packed), 1)
    return ((q == (i // cap) * SLOT_ROWS + part * cap + i % cap) & (i < used)).astype(BF16)


def middle_body(cap, block, used, own, where_ref, *refs):
    *bufs, wd_ref, act_ref, slope_ref, both_ref, own_ref, other_ref, dy, dyt = refs
    core = where_ref[1]
    packed, part = bufs[0].shape
    for p in range(PARTS):
        pick = picker(cap, block, used, packed, p)
        for j, buf in enumerate(bufs):
            dy[j * block : (j + 1) * block, p * part : (p + 1) * part] = jnp.dot(
                pick, buf[...], preferred_element_type=F32
            ).astype(BF16)
    hid = wd_ref.shape[0]
    d_hidden = lax.dot_general(dy[...], wd_ref[...], NT, preferred_element_type=F32)
    both_ref[:, :hid] = (d_hidden * slope_ref[...]).astype(BF16)
    both_ref[:, hid:] = (d_hidden * act_ref[...]).astype(BF16)
    one = eye()
    for t in range(dy.shape[1] // TILE):
        dyt[t * TILE : (t + 1) * TILE, :] = lax.dot_general(
            one, dy[:, t * TILE : (t + 1) * TILE], NT, preferred_element_type=F32
        ).astype(BF16)
    split_halves(dyt, core, own_ref, other_ref, own)


def back_body(cap, block, used, both_ref, wg_ref, wu_ref, *outs):
    packed, part = outs[0].shape
    hid = wg_ref.shape[0]
    step = part // 2
    picks = [picker(cap, block, used, packed, p) for p in range(PARTS)]
    d_gate = both_ref[:, :hid]
    d_up = both_ref[:, hid:]
    for h in range(part // step):
        pieces = []
        for p in range(PARTS):
            cols = slice(p * part + h * step, p * part + (h + 1) * step)
            pieces.append(
                (
                    jnp.dot(d_gate, wg_ref[:, cols], preferred_element_type=F32)
                    + jnp.dot(d_up, wu_ref[:, cols], preferred_element_type=F32)
                ).astype(BF16)
            )
        for j, out in enumerate(outs):
            total = None
            for p in range(PARTS):
                term = lax.dot_general(
                    picks[p], pieces[p][j * block : (j + 1) * block, :], TN, preferred_element_type=F32
                )
                total = term if total is None else total + term
            out[:, h * step : (h + 1) * step] = total.astype(BF16)


def terms_body(own, hid, xo, xp, yo, yp, do, dp, ho, hp, out):
    both = jnp.dot(xo[...], do[...], preferred_element_type=F32)
    both = both + jnp.dot(xp[...], dp[...], preferred_element_type=F32)
    down = jnp.dot(yo[...], ho[...], preferred_element_type=F32)
    down = down + jnp.dot(yp[...], hp[...], preferred_element_type=F32)
    both = both.astype(BF16)
    down = down.astype(BF16)
    for g in range(out.shape[0]):
        rows = slice(g * own, (g + 1) * own)
        out[g, 0] = both[rows, :hid]
        out[g, 1] = both[rows, hid:]
        out[g, 2] = down[rows, :]


def final_body(cap, routes_ref, back_ref, out_ref, sums, grads):
    depth = back_ref.shape[0] // EXPERTS
    tokens, width = out_ref.shape
    part = width // PARTS
    for e in range(EXPERTS):
        total = back_ref[e * depth].astype(F32)
        for k in range(1, depth):
            total = total + back_ref[e * depth + k].astype(F32)
        sums[e * SLOT_ROWS : (e + 1) * SLOT_ROWS, :] = total
    sums[EXPERTS * SLOT_ROWS :, :] = jnp.zeros((SLOT_ROWS, part), F32)
    held = [None, None]
    for token, choice, row in walk(routes_ref, tokens):
        held[choice] = row
        if choice == 1:
            for p in range(PARTS):
                grads[token : token + 1, p * part : (p + 1) * part] = (
                    sums[pl.ds(held[0] + p * cap, 1), :] + sums[pl.ds(held[1] + p * cap, 1), :]
                )
    out_ref[...] = grads[:tokens, :].astype(BF16)


def per_device(d_out, routes, probs, saved_inputs, w_gate, w_up, w_down):
    n_y, n_c, n_z, n_x = (lax.axis_size(a) for a in ("y", "c", "z", "x"))
    tokens, width = d_out.shape
    cap = tokens // 2
    hid = w_gate.shape[0]
    part = width // PARTS
    used = n_z * cap
    block = -(-used // 16) * 16
    rows = n_x * block
    packed = n_z * SLOT_ROWS
    own = width // (n_y * n_c)
    half = width // 2
    routes_t = routes.T
    probs_t = probs.T
    where = jnp.stack([lax.axis_index("x"), lax.axis_index("c")]).astype(jnp.int32)
    shape = jax.ShapeDtypeStruct
    x_in = saved_inputs.reshape(n_z * n_x * cap, width)

    sent = call(
        functools.partial(pack_body, cap),
        shape((n_z, SLOT_ROWS, part), BF16),
        [SMEM, SMEM, VMEM],
        [pltpu.VMEM(((EXPERTS + 1) * SLOT_ROWS, part), F32)],
        moved=500_000,
    )(routes_t, probs_t, d_out)
    first = lax.all_to_all(sent, "z", split_axis=0, concat_axis=0, tiled=True)

    x_own, x_other, act, slope, hidden = call(
        functools.partial(early_body, cap, n_x, block, own),
        (
            shape((half, rows), BF16),
            shape((half, rows), BF16),
            shape((rows, hid), F32),
            shape((rows, hid), F32),
            shape((rows, hid), BF16),
        ),
        [SMEM, VMEM, VMEM, VMEM],
        [pltpu.VMEM((rows, width), BF16), pltpu.VMEM((width, rows), BF16)],
        flops=2 * rows * width * (2 * hid + 2 * rows),
        moved=2 * width * (2 * hid + 2 * rows) + 10 * rows * hid,
    )(where, x_in, w_gate, w_up)

    def swap(v):
        return lax.ppermute(v, "c", [(i, (i + 1) % n_c) for i in range(n_c)])

    def shift(v, by):
        return lax.ppermute(v, "x", [(i, (i + by) % n_x) for i in range(n_x)])

    x_pair = swap(x_other)
    hidden_pair = swap(hidden)

    mine = first.reshape(packed, part)
    bufs = [mine] + [shift(mine, -j) for j in range(1, n_x)]
    both, y_own, y_other = call(
        functools.partial(middle_body, cap, block, used, own),
        (shape((rows, 2 * hid), BF16), shape((half, rows), BF16), shape((half, rows), BF16)),
        [SMEM] + [VMEM] * (n_x + 3),
        [pltpu.VMEM((rows, width), BF16), pltpu.VMEM((width, rows), BF16)],
        flops=2 * rows * width * (hid + rows),
        moved=2 * width * (hid + 2 * rows) + 10 * rows * hid,
    )(where, *bufs, w_down, act, slope)
    both_pair = swap(both)
    y_pair = swap(y_other)

    back = call(
        functools.partial(back_body, cap, block, used),
        tuple(shape((packed, part), BF16) for _ in range(n_x)),
        [VMEM] * 3,
        flops=2 * rows * width * 3 * hid,
        moved=2 * width * (2 * hid + rows),
    )(both, w_gate, w_up)

    steps = n_y // 2
    per = n_y // steps
    feature = pl.BlockSpec((per * own, rows), lambda g: (g, 0))
    whole = lambda n: pl.BlockSpec((rows, n), lambda g: (0, 0))
    terms = call(
        functools.partial(terms_body, own, hid),
        shape((n_y, 3, own, hid), BF16),
        [feature] * 4 + [whole(2 * hid)] * 2 + [whole(hid)] * 2,
        flops=2 * 2 * rows * half * 3 * hid,
        moved=2 * half * (3 * hid + 4 * rows),
        out_specs=pl.BlockSpec((per, 3, own, hid), lambda g: (g, 0, 0, 0)),
        grid=(steps,),
    )(x_own, x_pair, y_own, y_pair, both, both_pair, hidden, hidden_pair)
    shares = lax.psum_scatter(
        terms.reshape(n_y * 3 * own, hid), "y", scatter_dimension=0, tiled=True
    )
    weight_grads = shares.reshape(3, own, hid)

    arrived = [back[0]] + [shift(back[j], j) for j in range(1, n_x)]
    added = sum(v.astype(F32) for v in arrived).astype(BF16)
    returned = lax.all_to_all(
        added.reshape(n_z, SLOT_ROWS, part), "z", split_axis=0, concat_axis=0, tiled=True
    )
    input_grad = call(
        functools.partial(final_body, cap),
        shape((tokens, width), BF16),
        [SMEM, VMEM],
        [pltpu.VMEM(((EXPERTS + 1) * SLOT_ROWS, part), F32), pltpu.VMEM((16, width), F32)],
        moved=500_000,
    )(routes_t, returned)
    return (input_grad, weight_grads)


def solution(mesh):
    n_z = mesh.shape["expert"] // 4
    fine = Mesh(
        mesh.devices.reshape(mesh.shape["dp"] // 2, 2, n_z, 4), ("y", "c", "z", "x")
    )
    dp, expert = ("y", "c"), ("z", "x")
    every = dp + expert
    return jax.shard_map(
        per_device,
        mesh=fine,
        in_specs=(
            P(every, None),
            P(every, None),
            P(every, None),
            P(dp, expert, None, None),
            P(expert, None),
            P(expert, None),
            P(expert, None),
        ),
        out_specs=(P(every, None), P(None, dp, expert)),
        check_vma=False,
    )
```

```python
import functools

import jax
import jax.numpy as jnp
from jax import lax
from jax.experimental import pallas as pl
from jax.experimental.pallas import tpu as pltpu
from jax.sharding import Mesh, PartitionSpec as P

EXPERTS = 2
SLOT_ROWS = 16
PARTS = 3
TILE = 256
F32 = jnp.float32
BF16 = jnp.bfloat16
MIB = 1024 * 1024
NT = (((1,), (1,)), ((), ()))
TN = (((0,), (0,)), ((), ()))
VMEM = pl.BlockSpec(memory_space=pltpu.VMEM)
SMEM = pl.BlockSpec(memory_space=pltpu.SMEM)


def call(body, out_shape, in_specs, scratch=(), flops=0, moved=0, mib=16, **more):
    return pl.pallas_call(
        body,
        out_shape=out_shape,
        in_specs=in_specs,
        scratch_shapes=list(scratch),
        compiler_params=pltpu.CompilerParams(vmem_limit_bytes=mib * MIB),
        cost_estimate=pl.CostEstimate(flops=flops, bytes_accessed=moved, transcendentals=0),
        **more,
    )


def walk(routes_ref, tokens):
    counts = [jnp.int32(0)] * EXPERTS
    for token in range(tokens):
        for choice in range(2):
            expert = routes_ref[choice, token]
            row = jnp.int32(EXPERTS * SLOT_ROWS)
            for e in range(EXPERTS):
                here = expert == e
                row = jnp.where(here, e * SLOT_ROWS + counts[e], row)
                counts[e] = counts[e] + here.astype(jnp.int32)
            yield token, choice, row


def pack_body(cap, routes_ref, probs_ref, d_ref, out_ref, rows):
    tokens, width = d_ref.shape
    part = width // PARTS
    rows[...] = jnp.zeros_like(rows)
    d = d_ref[...].astype(F32)
    for token, choice, row in walk(routes_ref, tokens):
        scaled = probs_ref[choice, token] * d[token : token + 1, :]
        for p in range(PARTS):
            rows[pl.ds(row + p * cap, 1), :] = scaled[:, p * part : (p + 1) * part]
    depth = out_ref.shape[0] // EXPERTS
    for e in range(EXPERTS):
        block = rows[e * SLOT_ROWS : (e + 1) * SLOT_ROWS, :].astype(BF16)
        for k in range(depth):
            out_ref[e * depth + k] = block


def eye():
    i = lax.broadcasted_iota(jnp.int32, (TILE, TILE), 0)
    j = lax.broadcasted_iota(jnp.int32, (TILE, TILE), 1)
    return (i == j).astype(BF16)


def split_halves(full, core, own_ref, other_ref, own):
    groups = full.shape[0] // (2 * own)
    for g in range(groups):
        mine = pl.multiple_of(g * 2 * own + core * own, 16)
        theirs = pl.multiple_of(g * 2 * own + (1 - core) * own, 16)
        own_ref[g * own : (g + 1) * own, :] = full[pl.ds(mine, own), :]
        other_ref[g * own : (g + 1) * own, :] = full[pl.ds(theirs, own), :]


def early_body(cap, n_x, block, own, where_ref, x_ref, wg_ref, wu_ref, own_ref, other_ref, act_ref, slope_ref, hidden_ref, xp, xt):
    rows, width = xp.shape
    used = x_ref.shape[0] // n_x
    at = where_ref[0]
    core = where_ref[1]
    r = lax.broadcasted_iota(jnp.int32, (rows, x_ref.shape[0]), 0)
    q = lax.broadcasted_iota(jnp.int32, (rows, x_ref.shape[0]), 1)
    i = r % block
    source = (at + r // block) % n_x
    order = ((q == ((i // cap) * n_x + source) * cap + i % cap) & (i < used)).astype(BF16)
    one = eye()
    for t in range(width // TILE):
        piece = jnp.dot(order, x_ref[:, t * TILE : (t + 1) * TILE], preferred_element_type=F32).astype(BF16)
        xp[:, t * TILE : (t + 1) * TILE] = piece
        xt[t * TILE : (t + 1) * TILE, :] = lax.dot_general(one, piece, NT, preferred_element_type=F32).astype(BF16)
    split_halves(xt, core, own_ref, other_ref, own)
    gate = lax.dot_general(xp[...], wg_ref[...], NT, preferred_element_type=F32)
    upper = lax.dot_general(xp[...], wu_ref[...], NT, preferred_element_type=F32)
    sigma = jax.nn.sigmoid(gate)
    act = gate * sigma
    act_ref[...] = act
    slope_ref[...] = upper * sigma * (1.0 + gate * (1.0 - sigma))
    hidden_ref[...] = (act * upper).astype(BF16)


def picker(cap, block, used, packed, part):
    i = lax.broadcasted_iota(jnp.int32, (block, packed), 0)
    q = lax.broadcasted_iota(jnp.int32, (block, packed), 1)
    return ((q == (i // cap) * SLOT_ROWS + part * cap + i % cap) & (i < used)).astype(BF16)


def middle_body(cap, block, used, own, where_ref, *refs):
    *bufs, wd_ref, act_ref, slope_ref, ship_ref, own_ref, dy, dyt = refs
    core = where_ref[1]
    packed, part = bufs[0].shape
    hid, width = wd_ref.shape
    half = width // 2
    rows = dy.shape[0]
    for p in range(PARTS):
        pick = picker(cap, block, used, packed, p)
        for j, buf in enumerate(bufs):
            dy[j * block : (j + 1) * block, p * part : (p + 1) * part] = jnp.dot(
                pick, buf[...], preferred_element_type=F32
            ).astype(BF16)
    d_hidden = lax.dot_general(dy[...], wd_ref[...], NT, preferred_element_type=F32)
    both = jnp.concatenate([d_hidden * slope_ref[...], d_hidden * act_ref[...]], axis=1).astype(BF16)
    for k in range(2 * hid // rows):
        ship_ref[half + k * rows : half + (k + 1) * rows, :] = both[:, k * rows : (k + 1) * rows]
    one = eye()
    for t in range(width // TILE):
        dyt[t * TILE : (t + 1) * TILE, :] = lax.dot_general(
            one, dy[:, t * TILE : (t + 1) * TILE], NT, preferred_element_type=F32
        ).astype(BF16)
    split_halves(dyt, core, own_ref, ship_ref, own)


def columns(ref, first, rows, n):
    return [ref[first + k * rows : first + (k + 1) * rows, :] for k in range(n // rows)]


def back_body(block, both_ref, wg_ref, wu_ref, *outs):
    hid = wg_ref.shape[0]
    rows = both_ref.shape[1]
    both = jnp.concatenate(columns(both_ref, 0, rows, 2 * hid), axis=1)
    dx = jnp.dot(both[:, :hid], wg_ref[...], preferred_element_type=F32)
    dx = (dx + jnp.dot(both[:, hid:], wu_ref[...], preferred_element_type=F32)).astype(BF16)
    for j, out in enumerate(outs):
        out[...] = dx[j * block : (j + 1) * block, :]


def merge_body(cap, used, *refs):
    *bufs, out_ref, pack = refs
    block, width = bufs[0].shape
    depth = out_ref.shape[0]
    part = width // PARTS
    packed = depth * SLOT_ROWS
    i = lax.broadcasted_iota(jnp.int32, (packed, block), 1)
    q = lax.broadcasted_iota(jnp.int32, (packed, block), 0)
    for h in range(part // TILE):
        total = None
        for p in range(PARTS):
            cols = slice(p * part + h * TILE, p * part + (h + 1) * TILE)
            added = bufs[0][:, cols].astype(F32)
            for buf in bufs[1:]:
                added = added + buf[:, cols].astype(F32)
            put = ((q == (i // cap) * SLOT_ROWS + p * cap + i % cap) & (i < used)).astype(BF16)
            term = jnp.dot(put, added.astype(BF16), preferred_element_type=F32)
            total = term if total is None else total + term
        pack[:, h * TILE : (h + 1) * TILE] = total.astype(BF16)
    for k in range(depth):
        out_ref[k] = pack[k * SLOT_ROWS : (k + 1) * SLOT_ROWS, :]


def terms_body(own, hid, xo, xp, yo, yp, do, dp, ho, hp, out):
    rows = xo.shape[1]
    d_own = jnp.concatenate(columns(do, 0, rows, 2 * hid), axis=1)
    d_pair = jnp.concatenate(columns(dp, 0, rows, 2 * hid), axis=1)
    both = jnp.dot(xo[...], d_own, preferred_element_type=F32)
    both = both + jnp.dot(xp[...], d_pair, preferred_element_type=F32)
    down = jnp.dot(yo[...], ho[...], preferred_element_type=F32)
    down = down + jnp.dot(yp[...], hp[...], preferred_element_type=F32)
    both = both.astype(BF16)
    down = down.astype(BF16)
    for g in range(out.shape[0]):
        rows = slice(g * own, (g + 1) * own)
        out[g, 0] = both[rows, :hid]
        out[g, 1] = both[rows, hid:]
        out[g, 2] = down[rows, :]


def final_body(cap, routes_ref, back_ref, out_ref, sums, grads):
    depth = back_ref.shape[0] // EXPERTS
    tokens, width = out_ref.shape
    part = width // PARTS
    for e in range(EXPERTS):
        total = back_ref[e * depth].astype(F32)
        for k in range(1, depth):
            total = total + back_ref[e * depth + k].astype(F32)
        sums[e * SLOT_ROWS : (e + 1) * SLOT_ROWS, :] = total
    sums[EXPERTS * SLOT_ROWS :, :] = jnp.zeros((SLOT_ROWS, part), F32)
    held = [None, None]
    for token, choice, row in walk(routes_ref, tokens):
        held[choice] = row
        if choice == 1:
            for p in range(PARTS):
                grads[token : token + 1, p * part : (p + 1) * part] = (
                    sums[pl.ds(held[0] + p * cap, 1), :] + sums[pl.ds(held[1] + p * cap, 1), :]
                )
    out_ref[...] = grads[:tokens, :].astype(BF16)


def per_device(d_out, routes, probs, saved_inputs, w_gate, w_up, w_down):
    n_y, n_c, n_z, n_x = (lax.axis_size(a) for a in ("y", "c", "z", "x"))
    tokens, width = d_out.shape
    cap = tokens // 2
    hid = w_gate.shape[0]
    part = width // PARTS
    used = n_z * cap
    block = -(-used // 16) * 16
    rows = n_x * block
    packed = n_z * SLOT_ROWS
    own = width // (n_y * n_c)
    half = width // 2
    routes_t = routes.T
    probs_t = probs.T
    where = jnp.stack([lax.axis_index("x"), lax.axis_index("c")]).astype(jnp.int32)
    shape = jax.ShapeDtypeStruct
    x_in = saved_inputs.reshape(n_z * n_x * cap, width)

    sent = call(
        functools.partial(pack_body, cap),
        shape((n_z, SLOT_ROWS, part), BF16),
        [SMEM, SMEM, VMEM],
        [pltpu.VMEM(((EXPERTS + 1) * SLOT_ROWS, part), F32)],
        moved=500_000,
    )(routes_t, probs_t, d_out)
    first = lax.all_to_all(sent, "z", split_axis=0, concat_axis=0, tiled=True)

    x_own, x_other, act, slope, hidden = call(
        functools.partial(early_body, cap, n_x, block, own),
        (
            shape((half, rows), BF16),
            shape((half, rows), BF16),
            shape((rows, hid), F32),
            shape((rows, hid), F32),
            shape((rows, hid), BF16),
        ),
        [SMEM, VMEM, VMEM, VMEM],
        [pltpu.VMEM((rows, width), BF16), pltpu.VMEM((width, rows), BF16)],
        mib=24,
        flops=2 * rows * width * (2 * hid + 2 * rows),
        moved=2 * width * (2 * hid + 2 * rows) + 10 * rows * hid,
    )(where, x_in, w_gate, w_up)

    def swap(v):
        return lax.ppermute(v, "c", [(i, (i + 1) % n_c) for i in range(n_c)])

    def shift(v, by):
        return lax.ppermute(v, "x", [(i, (i + by) % n_x) for i in range(n_x)])

    x_pair = swap(x_other)
    hidden_pair = swap(hidden)
    first, x_pair, hidden_pair = lax.optimization_barrier((first, x_pair, hidden_pair))

    mine = first.reshape(packed, part)
    bufs = [mine] + [shift(mine, -j) for j in range(1, n_x)]
    ship, y_own = call(
        functools.partial(middle_body, cap, block, used, own),
        (shape((half + 2 * hid, rows), BF16), shape((half, rows), BF16)),
        [SMEM] + [VMEM] * (n_x + 3),
        [pltpu.VMEM((rows, width), BF16), pltpu.VMEM((width, rows), BF16)],
        flops=2 * rows * width * (hid + rows),
        moved=2 * width * (hid + 2 * rows) + 10 * rows * hid,
    )(where, *bufs, w_down, act, slope)
    got = swap(ship)

    step = 512
    late = half // (2 * hid)
    back = call(
        functools.partial(back_body, block),
        tuple(shape((block, width), BF16) for _ in range(n_x)),
        [pl.BlockSpec((2 * hid, rows), lambda g: (late, 0))] + [pl.BlockSpec((hid, step), lambda g: (0, g))] * 2,
        flops=2 * rows * width * 2 * hid,
        moved=2 * width * (2 * hid + rows),
        out_specs=tuple(pl.BlockSpec((block, step), lambda g: (0, g)) for _ in range(n_x)),
        grid=(width // step,),
    )(ship, w_gate, w_up)
    got, back = lax.optimization_barrier((got, back))

    steps = n_y // 2
    per = n_y // steps
    feature = pl.BlockSpec((per * own, rows), lambda g: (g, 0))
    tail = pl.BlockSpec((2 * hid, rows), lambda g: (late, 0))
    whole = pl.BlockSpec((rows, hid), lambda g: (0, 0))
    terms = call(
        functools.partial(terms_body, own, hid),
        shape((n_y, 3, own, hid), BF16),
        [feature] * 4 + [tail] * 2 + [whole] * 2,
        flops=2 * 2 * rows * half * 3 * hid,
        moved=2 * half * (3 * hid + 4 * rows),
        out_specs=pl.BlockSpec((per, 3, own, hid), lambda g: (g, 0, 0, 0)),
        grid=(steps,),
    )(x_own, x_pair, y_own, got, ship, got, hidden, hidden_pair)
    shares = lax.psum_scatter(
        terms.reshape(n_y * 3 * own, hid), "y", scatter_dimension=0, tiled=True
    )
    weight_grads = shares.reshape(3, own, hid)

    arrived = [back[0]] + [shift(back[j], j) for j in range(1, n_x)]
    added = call(
        functools.partial(merge_body, cap, used),
        shape((n_z, SLOT_ROWS, part), BF16),
        [VMEM] * n_x,
        [pltpu.VMEM((packed, part), BF16)],
        flops=2 * packed * block * width,
        moved=2 * n_x * block * width,
    )(*arrived)
    returned = lax.all_to_all(
        added, "z", split_axis=0, concat_axis=0, tiled=True
    )
    input_grad = call(
        functools.partial(final_body, cap),
        shape((tokens, width), BF16),
        [SMEM, VMEM],
        [pltpu.VMEM(((EXPERTS + 1) * SLOT_ROWS, part), F32), pltpu.VMEM((16, width), F32)],
        moved=500_000,
    )(routes_t, returned)
    return (input_grad, weight_grads)


def solution(mesh):
    n_z = mesh.shape["expert"] // 4
    fine = Mesh(
        mesh.devices.reshape(mesh.shape["dp"] // 2, 2, n_z, 4), ("y", "c", "z", "x")
    )
    dp, expert = ("y", "c"), ("z", "x")
    every = dp + expert
    return jax.shard_map(
        per_device,
        mesh=fine,
        in_specs=(
            P(every, None),
            P(every, None),
            P(every, None),
            P(dp, expert, None, None),
            P(expert, None),
            P(expert, None),
            P(expert, None),
        ),
        out_specs=(P(every, None), P(None, dp, expert)),
        check_vma=False,
    )
```

```python
import functools

import jax
import jax.numpy as jnp
from jax import lax
from jax.experimental import pallas as pl
from jax.experimental.pallas import tpu as pltpu
from jax.sharding import Mesh, PartitionSpec as P

EXPERTS = 2
SLOT_ROWS = 16
PARTS = 3
TILE = 256
F32 = jnp.float32
BF16 = jnp.bfloat16
MIB = 1024 * 1024
NT = (((1,), (1,)), ((), ()))
TN = (((0,), (0,)), ((), ()))
VMEM = pl.BlockSpec(memory_space=pltpu.VMEM)
SMEM = pl.BlockSpec(memory_space=pltpu.SMEM)
HBM = pl.BlockSpec(memory_space=pltpu.HBM)


def call(body, out_shape, in_specs, scratch=(), flops=0, moved=0, mib=16, **more):
    return pl.pallas_call(
        body,
        out_shape=out_shape,
        in_specs=in_specs,
        scratch_shapes=list(scratch),
        compiler_params=pltpu.CompilerParams(vmem_limit_bytes=mib * MIB),
        cost_estimate=pl.CostEstimate(flops=flops, bytes_accessed=moved, transcendentals=0),
        **more,
    )


def walk(routes_ref, tokens):
    counts = [jnp.int32(0)] * EXPERTS
    for token in range(tokens):
        for choice in range(2):
            expert = routes_ref[choice, token]
            row = jnp.int32(EXPERTS * SLOT_ROWS)
            for e in range(EXPERTS):
                here = expert == e
                row = jnp.where(here, e * SLOT_ROWS + counts[e], row)
                counts[e] = counts[e] + here.astype(jnp.int32)
            yield token, choice, row


def pack_body(cap, routes_ref, probs_ref, d_ref, out_ref, rows):
    tokens, width = d_ref.shape
    part = width // PARTS
    rows[...] = jnp.zeros_like(rows)
    d = d_ref[...].astype(F32)
    for token, choice, row in walk(routes_ref, tokens):
        scaled = probs_ref[choice, token] * d[token : token + 1, :]
        for p in range(PARTS):
            rows[pl.ds(row + p * cap, 1), :] = scaled[:, p * part : (p + 1) * part]
    depth = out_ref.shape[0] // EXPERTS
    for e in range(EXPERTS):
        block = rows[e * SLOT_ROWS : (e + 1) * SLOT_ROWS, :].astype(BF16)
        for k in range(depth):
            out_ref[e * depth + k] = block


def eye():
    i = lax.broadcasted_iota(jnp.int32, (TILE, TILE), 0)
    j = lax.broadcasted_iota(jnp.int32, (TILE, TILE), 1)
    return (i == j).astype(BF16)


def split_halves(full, core, own_ref, other_ref, own):
    groups = full.shape[0] // (2 * own)
    for g in range(groups):
        mine = pl.multiple_of(g * 2 * own + core * own, 16)
        theirs = pl.multiple_of(g * 2 * own + (1 - core) * own, 16)
        own_ref[g * own : (g + 1) * own, :] = full[pl.ds(mine, own), :]
        other_ref[g * own : (g + 1) * own, :] = full[pl.ds(theirs, own), :]


def start_all(pairs, sems, first=0):
    copies = [pltpu.make_async_copy(a, b, sems.at[first + n]) for n, (a, b) in enumerate(pairs)]
    for copy in copies:
        copy.start()
    return copies


def early_body(cap, n_x, block, own, where_ref, x_at, wg_at, wu_at, own_at, other_at, act_at, slope_at, hidden_at, *scratch):
    xp, xt, x_ref, wg_ref, wu_ref, own_ref, other_ref, act_ref, slope_ref, hidden_ref, sems = scratch
    fetches = start_all(((x_at, x_ref), (wg_at, wg_ref), (wu_at, wu_ref)), sems)
    rows, width = xp.shape
    used = x_ref.shape[0] // n_x
    at = where_ref[0]
    core = where_ref[1]
    r = lax.broadcasted_iota(jnp.int32, (rows, x_ref.shape[0]), 0)
    q = lax.broadcasted_iota(jnp.int32, (rows, x_ref.shape[0]), 1)
    i = r % block
    source = (at + r // block) % n_x
    order = ((q == ((i // cap) * n_x + source) * cap + i % cap) & (i < used)).astype(BF16)
    one = eye()
    fetches[0].wait()
    for t in range(width // TILE):
        piece = jnp.dot(order, x_ref[:, t * TILE : (t + 1) * TILE], preferred_element_type=F32).astype(BF16)
        xp[:, t * TILE : (t + 1) * TILE] = piece
        xt[t * TILE : (t + 1) * TILE, :] = lax.dot_general(one, piece, NT, preferred_element_type=F32).astype(BF16)
    split_halves(xt, core, own_ref, other_ref, own)
    stores = start_all(((other_ref, other_at), (own_ref, own_at)), sems, 3)
    fetches[1].wait()
    gate = lax.dot_general(xp[...], wg_ref[...], NT, preferred_element_type=F32)
    fetches[2].wait()
    upper = lax.dot_general(xp[...], wu_ref[...], NT, preferred_element_type=F32)
    sigma = jax.nn.sigmoid(gate)
    act = gate * sigma
    act_ref[...] = act
    slope_ref[...] = upper * sigma * (1.0 + gate * (1.0 - sigma))
    hidden_ref[...] = (act * upper).astype(BF16)
    stores += start_all(((hidden_ref, hidden_at), (act_ref, act_at), (slope_ref, slope_at)), sems, 5)
    for store in stores:
        store.wait()


def picker(cap, block, used, packed, part):
    i = lax.broadcasted_iota(jnp.int32, (block, packed), 0)
    q = lax.broadcasted_iota(jnp.int32, (block, packed), 1)
    return ((q == (i // cap) * SLOT_ROWS + part * cap + i % cap) & (i < used)).astype(BF16)


def middle_body(cap, block, used, own, where_ref, *refs):
    *bufs, wd_at, act_at, slope_at, ship_ref, own_ref, dy, dyt, wd_ref, act_ref, slope_ref, arrived = refs
    fetches = start_all(((wd_at, wd_ref), (act_at, act_ref), (slope_at, slope_ref)), arrived)
    core = where_ref[1]
    packed, part = bufs[0].shape
    hid, width = wd_ref.shape
    half = width // 2
    rows = dy.shape[0]
    for p in range(PARTS):
        pick = picker(cap, block, used, packed, p)
        for j, buf in enumerate(bufs):
            dy[j * block : (j + 1) * block, p * part : (p + 1) * part] = jnp.dot(
                pick, buf[...], preferred_element_type=F32
            ).astype(BF16)
    fetches[0].wait()
    d_hidden = lax.dot_general(dy[...], wd_ref[...], NT, preferred_element_type=F32)
    fetches[1].wait()
    fetches[2].wait()
    both = jnp.concatenate([d_hidden * slope_ref[...], d_hidden * act_ref[...]], axis=1).astype(BF16)
    for k in range(2 * hid // rows):
        ship_ref[half + k * rows : half + (k + 1) * rows, :] = both[:, k * rows : (k + 1) * rows]
    one = eye()
    for t in range(width // TILE):
        dyt[t * TILE : (t + 1) * TILE, :] = lax.dot_general(
            one, dy[:, t * TILE : (t + 1) * TILE], NT, preferred_element_type=F32
        ).astype(BF16)
    split_halves(dyt, core, own_ref, ship_ref, own)


def columns(ref, first, rows, n):
    return [ref[first + k * rows : first + (k + 1) * rows, :] for k in range(n // rows)]


def back_body(block, both_ref, wg_ref, wu_ref, *outs):
    hid = wg_ref.shape[0]
    rows = both_ref.shape[1]
    both = jnp.concatenate(columns(both_ref, 0, rows, 2 * hid), axis=1)
    dx = jnp.dot(both[:, :hid], wg_ref[...], preferred_element_type=F32)
    dx = (dx + jnp.dot(both[:, hid:], wu_ref[...], preferred_element_type=F32)).astype(BF16)
    for j, out in enumerate(outs):
        out[...] = dx[j * block : (j + 1) * block, :]


def merge_body(cap, used, *refs):
    *bufs, out_ref, pack = refs
    block, width = bufs[0].shape
    depth = out_ref.shape[0]
    part = width // PARTS
    packed = depth * SLOT_ROWS
    i = lax.broadcasted_iota(jnp.int32, (packed, block), 1)
    q = lax.broadcasted_iota(jnp.int32, (packed, block), 0)
    for h in range(part // TILE):
        total = None
        for p in range(PARTS):
            cols = slice(p * part + h * TILE, p * part + (h + 1) * TILE)
            added = bufs[0][:, cols].astype(F32)
            for buf in bufs[1:]:
                added = added + buf[:, cols].astype(F32)
            put = ((q == (i // cap) * SLOT_ROWS + p * cap + i % cap) & (i < used)).astype(BF16)
            term = jnp.dot(put, added.astype(BF16), preferred_element_type=F32)
            total = term if total is None else total + term
        pack[:, h * TILE : (h + 1) * TILE] = total.astype(BF16)
    for k in range(depth):
        out_ref[k] = pack[k * SLOT_ROWS : (k + 1) * SLOT_ROWS, :]


def terms_body(own, hid, xo, xp, yo, yp, do, dp, ho, hp, out):
    rows = xo.shape[1]
    d_own = jnp.concatenate(columns(do, 0, rows, 2 * hid), axis=1)
    d_pair = jnp.concatenate(columns(dp, 0, rows, 2 * hid), axis=1)
    both = jnp.dot(xo[...], d_own, preferred_element_type=F32)
    both = both + jnp.dot(xp[...], d_pair, preferred_element_type=F32)
    down = jnp.dot(yo[...], ho[...], preferred_element_type=F32)
    down = down + jnp.dot(yp[...], hp[...], preferred_element_type=F32)
    both = both.astype(BF16)
    down = down.astype(BF16)
    for g in range(out.shape[0]):
        rows = slice(g * own, (g + 1) * own)
        out[g, 0] = both[rows, :hid]
        out[g, 1] = both[rows, hid:]
        out[g, 2] = down[rows, :]


def final_body(cap, routes_ref, back_ref, out_ref, sums, grads):
    depth = back_ref.shape[0] // EXPERTS
    tokens, width = out_ref.shape
    part = width // PARTS
    for e in range(EXPERTS):
        total = back_ref[e * depth].astype(F32)
        for k in range(1, depth):
            total = total + back_ref[e * depth + k].astype(F32)
        sums[e * SLOT_ROWS : (e + 1) * SLOT_ROWS, :] = total
    sums[EXPERTS * SLOT_ROWS :, :] = jnp.zeros((SLOT_ROWS, part), F32)
    held = [None, None]
    for token, choice, row in walk(routes_ref, tokens):
        held[choice] = row
        if choice == 1:
            for p in range(PARTS):
                grads[token : token + 1, p * part : (p + 1) * part] = (
                    sums[pl.ds(held[0] + p * cap, 1), :] + sums[pl.ds(held[1] + p * cap, 1), :]
                )
    out_ref[...] = grads[:tokens, :].astype(BF16)


def per_device(d_out, routes, probs, saved_inputs, w_gate, w_up, w_down):
    n_y, n_c, n_z, n_x = (lax.axis_size(a) for a in ("y", "c", "z", "x"))
    tokens, width = d_out.shape
    cap = tokens // 2
    hid = w_gate.shape[0]
    part = width // PARTS
    used = n_z * cap
    block = -(-used // 16) * 16
    rows = n_x * block
    packed = n_z * SLOT_ROWS
    own = width // (n_y * n_c)
    half = width // 2
    routes_t = routes.T
    probs_t = probs.T
    where = jnp.stack([lax.axis_index("x"), lax.axis_index("c")]).astype(jnp.int32)
    shape = jax.ShapeDtypeStruct
    x_in = saved_inputs.reshape(n_z * n_x * cap, width)

    sent = call(
        functools.partial(pack_body, cap),
        shape((n_z, SLOT_ROWS, part), BF16),
        [SMEM, SMEM, VMEM],
        [pltpu.VMEM(((EXPERTS + 1) * SLOT_ROWS, part), F32)],
        moved=500_000,
        mib=56,
    )(routes_t, probs_t, d_out)
    first = lax.all_to_all(sent, "z", split_axis=0, concat_axis=0, tiled=True)

    x_own, x_other, act, slope, hidden = call(
        functools.partial(early_body, cap, n_x, block, own),
        (
            shape((half, rows), BF16),
            shape((half, rows), BF16),
            shape((rows, hid), F32),
            shape((rows, hid), F32),
            shape((rows, hid), BF16),
        ),
        [SMEM, HBM, HBM, HBM],
        [
            pltpu.VMEM((rows, width), BF16),
            pltpu.VMEM((width, rows), BF16),
            pltpu.VMEM(x_in.shape, BF16),
            pltpu.VMEM(w_gate.shape, BF16),
            pltpu.VMEM(w_up.shape, BF16),
            pltpu.VMEM((half, rows), BF16),
            pltpu.VMEM((half, rows), BF16),
            pltpu.VMEM((rows, hid), F32),
            pltpu.VMEM((rows, hid), F32),
            pltpu.VMEM((rows, hid), BF16),
            pltpu.SemaphoreType.DMA((8,)),
        ],
        mib=60,
        out_specs=(HBM,) * 5,
        flops=2 * rows * width * (2 * hid + 2 * rows),
        moved=2 * width * (2 * hid + 2 * rows) + 10 * rows * hid,
    )(where, x_in, w_gate, w_up)

    def swap(v):
        return lax.ppermute(v, "c", [(i, (i + 1) % n_c) for i in range(n_c)])

    def shift(v, by):
        return lax.ppermute(v, "x", [(i, (i + by) % n_x) for i in range(n_x)])

    x_pair = swap(x_other)
    hidden_pair = swap(hidden)

    first, x_pair, hidden_pair = lax.optimization_barrier((first, x_pair, hidden_pair))
    mine = first.reshape(packed, part)
    bufs = [mine] + [shift(mine, -j) for j in range(1, n_x)]
    ship, y_own = call(
        functools.partial(middle_body, cap, block, used, own),
        (shape((half + 2 * hid, rows), BF16), shape((half, rows), BF16)),
        [SMEM] + [VMEM] * n_x + [HBM] * 3,
        [
            pltpu.VMEM((rows, width), BF16),
            pltpu.VMEM((width, rows), BF16),
            pltpu.VMEM(w_down.shape, BF16),
            pltpu.VMEM((rows, hid), F32),
            pltpu.VMEM((rows, hid), F32),
            pltpu.SemaphoreType.DMA((3,)),
        ],
        mib=16,
        flops=2 * rows * width * (hid + rows),
        moved=2 * width * (hid + 2 * rows) + 10 * rows * hid,
    )(where, *bufs, w_down, act, slope)
    got = swap(ship)

    step = 512
    late = half // (2 * hid)
    back = call(
        functools.partial(back_body, block),
        tuple(shape((block, width), BF16) for _ in range(n_x)),
        [pl.BlockSpec((2 * hid, rows), lambda g: (late, 0))] + [pl.BlockSpec((hid, step), lambda g: (0, g))] * 2,
        flops=2 * rows * width * 2 * hid,
        moved=2 * width * (2 * hid + rows),
        out_specs=tuple(pl.BlockSpec((block, step), lambda g: (0, g)) for _ in range(n_x)),
        grid=(width // step,),
    )(ship, w_gate, w_up)
    got, back = lax.optimization_barrier((got, back))

    steps = n_y // 2
    per = n_y // steps
    feature = pl.BlockSpec((per * own, rows), lambda g: (g, 0))
    tail = pl.BlockSpec((2 * hid, rows), lambda g: (late, 0))
    whole = pl.BlockSpec((rows, hid), lambda g: (0, 0))
    terms = call(
        functools.partial(terms_body, own, hid),
        shape((n_y, 3, own, hid), BF16),
        [feature] * 4 + [tail] * 2 + [whole] * 2,
        flops=2 * 2 * rows * half * 3 * hid,
        moved=2 * half * (3 * hid + 4 * rows),
        out_specs=pl.BlockSpec((per, 3, own, hid), lambda g: (g, 0, 0, 0)),
        grid=(steps,),
    )(x_own, x_pair, y_own, got, ship, got, hidden, hidden_pair)
    shares = lax.psum_scatter(
        terms.reshape(n_y * 3 * own, hid), "y", scatter_dimension=0, tiled=True
    )
    weight_grads = shares.reshape(3, own, hid)

    arrived = [back[0]] + [shift(back[j], j) for j in range(1, n_x)]
    added = call(
        functools.partial(merge_body, cap, used),
        shape((n_z, SLOT_ROWS, part), BF16),
        [VMEM] * n_x,
        [pltpu.VMEM((packed, part), BF16)],
        flops=2 * packed * block * width,
        moved=2 * n_x * block * width,
    )(*arrived)
    returned = lax.all_to_all(
        added, "z", split_axis=0, concat_axis=0, tiled=True
    )
    input_grad = call(
        functools.partial(final_body, cap),
        shape((tokens, width), BF16),
        [SMEM, VMEM],
        [pltpu.VMEM(((EXPERTS + 1) * SLOT_ROWS, part), F32), pltpu.VMEM((16, width), F32)],
        moved=500_000,
    )(routes_t, returned)
    return (input_grad, weight_grads)


def solution(mesh):
    n_z = mesh.shape["expert"] // 4
    fine = Mesh(
        mesh.devices.reshape(mesh.shape["dp"] // 2, 2, n_z, 4), ("y", "c", "z", "x")
    )
    dp, expert = ("y", "c"), ("z", "x")
    every = dp + expert
    return jax.shard_map(
        per_device,
        mesh=fine,
        in_specs=(
            P(every, None),
            P(every, None),
            P(every, None),
            P(dp, expert, None, None),
            P(expert, None),
            P(expert, None),
            P(expert, None),
        ),
        out_specs=(P(every, None), P(None, dp, expert)),
        check_vma=False,
    )
```

```python
import functools

import jax
import jax.numpy as jnp
from jax import lax
from jax.experimental import pallas as pl
from jax.experimental.pallas import tpu as pltpu
from jax.sharding import Mesh, PartitionSpec as P

EXPERTS = 2
SLOT_ROWS = 16
PARTS = 3
TILE = 256
F32 = jnp.float32
BF16 = jnp.bfloat16
MIB = 1024 * 1024
NT = (((1,), (1,)), ((), ()))
TN = (((0,), (0,)), ((), ()))
VMEM = pl.BlockSpec(memory_space=pltpu.VMEM)
SMEM = pl.BlockSpec(memory_space=pltpu.SMEM)
HBM = pl.BlockSpec(memory_space=pltpu.HBM)


def call(body, out_shape, in_specs, scratch=(), flops=0, moved=0, mib=16, **more):
    return pl.pallas_call(
        body,
        out_shape=out_shape,
        in_specs=in_specs,
        scratch_shapes=list(scratch),
        compiler_params=pltpu.CompilerParams(vmem_limit_bytes=mib * MIB),
        cost_estimate=pl.CostEstimate(flops=flops, bytes_accessed=moved, transcendentals=0),
        **more,
    )


def walk(routes_ref, tokens):
    counts = [jnp.int32(0)] * EXPERTS
    for token in range(tokens):
        for choice in range(2):
            expert = routes_ref[choice, token]
            row = jnp.int32(EXPERTS * SLOT_ROWS)
            for e in range(EXPERTS):
                here = expert == e
                row = jnp.where(here, e * SLOT_ROWS + counts[e], row)
                counts[e] = counts[e] + here.astype(jnp.int32)
            yield token, choice, row


def pack_body(cap, routes_ref, probs_ref, d_ref, out_ref, rows):
    tokens, width = d_ref.shape
    part = width // PARTS
    rows[...] = jnp.zeros_like(rows)
    d = d_ref[...].astype(F32)
    for token, choice, row in walk(routes_ref, tokens):
        scaled = probs_ref[choice, token] * d[token : token + 1, :]
        for p in range(PARTS):
            rows[pl.ds(row + p * cap, 1), :] = scaled[:, p * part : (p + 1) * part]
    depth = out_ref.shape[0] // EXPERTS
    for e in range(EXPERTS):
        block = rows[e * SLOT_ROWS : (e + 1) * SLOT_ROWS, :].astype(BF16)
        for k in range(depth):
            out_ref[e * depth + k] = block


def eye():
    i = lax.broadcasted_iota(jnp.int32, (TILE, TILE), 0)
    j = lax.broadcasted_iota(jnp.int32, (TILE, TILE), 1)
    return (i == j).astype(BF16)


def split_halves(full, core, own_ref, other_ref, own):
    groups = full.shape[0] // (2 * own)
    for g in range(groups):
        mine = pl.multiple_of(g * 2 * own + core * own, 16)
        theirs = pl.multiple_of(g * 2 * own + (1 - core) * own, 16)
        own_ref[g * own : (g + 1) * own, :] = full[pl.ds(mine, own), :]
        other_ref[g * own : (g + 1) * own, :] = full[pl.ds(theirs, own), :]


def start_all(pairs, sems, first=0):
    copies = [pltpu.make_async_copy(a, b, sems.at[first + n]) for n, (a, b) in enumerate(pairs)]
    for copy in copies:
        copy.start()
    return copies


def early_body(cap, n_x, block, own, where_ref, x_at, wg_at, wu_at, own_at, other_at, act_at, slope_at, hidden_at, *scratch):
    xp, xt, x_ref, wg_ref, wu_ref, own_ref, other_ref, act_ref, slope_ref, hidden_ref, sems = scratch
    fetches = start_all(((x_at, x_ref), (wg_at, wg_ref), (wu_at, wu_ref)), sems)
    rows, width = xp.shape
    used = x_ref.shape[0] // n_x
    at = where_ref[0]
    core = where_ref[1]
    r = lax.broadcasted_iota(jnp.int32, (rows, x_ref.shape[0]), 0)
    q = lax.broadcasted_iota(jnp.int32, (rows, x_ref.shape[0]), 1)
    i = r % block
    source = (at + r // block) % n_x
    order = ((q == ((i // cap) * n_x + source) * cap + i % cap) & (i < used)).astype(BF16)
    one = eye()
    fetches[0].wait()
    for t in range(width // TILE):
        piece = jnp.dot(order, x_ref[:, t * TILE : (t + 1) * TILE], preferred_element_type=F32).astype(BF16)
        xp[:, t * TILE : (t + 1) * TILE] = piece
        xt[t * TILE : (t + 1) * TILE, :] = lax.dot_general(one, piece, NT, preferred_element_type=F32).astype(BF16)
    split_halves(xt, core, own_ref, other_ref, own)
    stores = start_all(((other_ref, other_at), (own_ref, own_at)), sems, 3)
    fetches[1].wait()
    gate = lax.dot_general(xp[...], wg_ref[...], NT, preferred_element_type=F32)
    fetches[2].wait()
    upper = lax.dot_general(xp[...], wu_ref[...], NT, preferred_element_type=F32)
    sigma = jax.nn.sigmoid(gate)
    act = gate * sigma
    act_ref[...] = act
    slope_ref[...] = upper * sigma * (1.0 + gate * (1.0 - sigma))
    hidden_ref[...] = (act * upper).astype(BF16)
    stores += start_all(((hidden_ref, hidden_at), (act_ref, act_at), (slope_ref, slope_at)), sems, 5)
    for store in stores:
        store.wait()


def hold_body(act_at, slope_at, act_ref, slope_ref, sems):
    for copy in start_all(((act_at, act_ref), (slope_at, slope_ref)), sems):
        copy.wait()


def picker(cap, block, used, packed, part):
    i = lax.broadcasted_iota(jnp.int32, (block, packed), 0)
    q = lax.broadcasted_iota(jnp.int32, (block, packed), 1)
    return ((q == (i // cap) * SLOT_ROWS + part * cap + i % cap) & (i < used)).astype(BF16)


def middle_body(cap, block, used, own, where_ref, *refs):
    *bufs, wd_ref, act_ref, slope_ref, ship_ref, own_ref, dy, dyt = refs
    core = where_ref[1]
    packed, part = bufs[0].shape
    hid, width = wd_ref.shape
    half = width // 2
    rows = dy.shape[0]
    for p in range(PARTS):
        pick = picker(cap, block, used, packed, p)
        for j, buf in enumerate(bufs):
            dy[j * block : (j + 1) * block, p * part : (p + 1) * part] = jnp.dot(
                pick, buf[...], preferred_element_type=F32
            ).astype(BF16)
    d_hidden = lax.dot_general(dy[...], wd_ref[...], NT, preferred_element_type=F32)
    both = jnp.concatenate([d_hidden * slope_ref[...], d_hidden * act_ref[...]], axis=1).astype(BF16)
    for k in range(2 * hid // rows):
        ship_ref[half + k * rows : half + (k + 1) * rows, :] = both[:, k * rows : (k + 1) * rows]
    one = eye()
    for t in range(width // TILE):
        dyt[t * TILE : (t + 1) * TILE, :] = lax.dot_general(
            one, dy[:, t * TILE : (t + 1) * TILE], NT, preferred_element_type=F32
        ).astype(BF16)
    split_halves(dyt, core, own_ref, ship_ref, own)


def columns(ref, first, rows, n):
    return [ref[first + k * rows : first + (k + 1) * rows, :] for k in range(n // rows)]


def back_body(block, first, ship_ref, wg_ref, wu_ref, *outs):
    hid, width = wg_ref.shape
    step = 2 * TILE
    both = jnp.concatenate(columns(ship_ref, first, ship_ref.shape[1], 2 * hid), axis=1)
    for t in range(width // step):
        cols = slice(t * step, (t + 1) * step)
        dx = jnp.dot(both[:, :hid], wg_ref[:, cols], preferred_element_type=F32)
        dx = (dx + jnp.dot(both[:, hid:], wu_ref[:, cols], preferred_element_type=F32)).astype(BF16)
        for j, out in enumerate(outs):
            out[:, cols] = dx[j * block : (j + 1) * block, :]


def merge_body(cap, used, *refs):
    *bufs, out_ref, pack = refs
    block, width = bufs[0].shape
    depth = out_ref.shape[0]
    part = width // PARTS
    packed = depth * SLOT_ROWS
    i = lax.broadcasted_iota(jnp.int32, (packed, block), 1)
    q = lax.broadcasted_iota(jnp.int32, (packed, block), 0)
    for h in range(part // TILE):
        total = None
        for p in range(PARTS):
            cols = slice(p * part + h * TILE, p * part + (h + 1) * TILE)
            added = bufs[0][:, cols].astype(F32)
            for buf in bufs[1:]:
                added = added + buf[:, cols].astype(F32)
            put = ((q == (i // cap) * SLOT_ROWS + p * cap + i % cap) & (i < used)).astype(BF16)
            term = jnp.dot(put, added.astype(BF16), preferred_element_type=F32)
            total = term if total is None else total + term
        pack[:, h * TILE : (h + 1) * TILE] = total.astype(BF16)
    for k in range(depth):
        out_ref[k] = pack[k * SLOT_ROWS : (k + 1) * SLOT_ROWS, :]


def terms_body(own, hid, steps, xo, xp, yo, ship, got, ho, hp, out_at, stage, sems):
    half, rows = xo.shape
    per = out_at.shape[0] // steps
    depth = per * own
    d_own = jnp.concatenate(columns(ship, half, rows, 2 * hid), axis=1)
    d_pair = jnp.concatenate(columns(got, half, rows, 2 * hid), axis=1)
    stores = []
    for s in range(steps):
        here = slice(s * depth, (s + 1) * depth)
        both = jnp.dot(xo[here, :], d_own, preferred_element_type=F32)
        both = (both + jnp.dot(xp[here, :], d_pair, preferred_element_type=F32)).astype(BF16)
        down = jnp.dot(yo[here, :], ho[...], preferred_element_type=F32)
        down = (down + jnp.dot(got[here, :], hp[...], preferred_element_type=F32)).astype(BF16)
        for g in range(per):
            part = slice(g * own, (g + 1) * own)
            stage[s * per + g, 0] = both[part, :hid]
            stage[s * per + g, 1] = both[part, hid:]
            stage[s * per + g, 2] = down[part, :]
        groups = pl.ds(s * per, per)
        stores += start_all(((stage.at[groups], out_at.at[groups]),), sems, s)
    for store in stores:
        store.wait()


def final_body(cap, routes_ref, back_ref, out_ref, sums, grads):
    depth = back_ref.shape[0] // EXPERTS
    tokens, width = out_ref.shape
    part = width // PARTS
    for e in range(EXPERTS):
        total = back_ref[e * depth].astype(F32)
        for k in range(1, depth):
            total = total + back_ref[e * depth + k].astype(F32)
        sums[e * SLOT_ROWS : (e + 1) * SLOT_ROWS, :] = total
    sums[EXPERTS * SLOT_ROWS :, :] = jnp.zeros((SLOT_ROWS, part), F32)
    held = [None, None]
    for token, choice, row in walk(routes_ref, tokens):
        held[choice] = row
        if choice == 1:
            for p in range(PARTS):
                grads[token : token + 1, p * part : (p + 1) * part] = (
                    sums[pl.ds(held[0] + p * cap, 1), :] + sums[pl.ds(held[1] + p * cap, 1), :]
                )
    out_ref[...] = grads[:tokens, :].astype(BF16)


def per_device(d_out, routes, probs, saved_inputs, w_gate, w_up, w_down):
    n_y, n_c, n_z, n_x = (lax.axis_size(a) for a in ("y", "c", "z", "x"))
    tokens, width = d_out.shape
    cap = tokens // 2
    hid = w_gate.shape[0]
    part = width // PARTS
    used = n_z * cap
    block = -(-used // 16) * 16
    rows = n_x * block
    packed = n_z * SLOT_ROWS
    own = width // (n_y * n_c)
    half = width // 2
    routes_t = routes.T
    probs_t = probs.T
    where = jnp.stack([lax.axis_index("x"), lax.axis_index("c")]).astype(jnp.int32)
    shape = jax.ShapeDtypeStruct
    x_in = saved_inputs.reshape(n_z * n_x * cap, width)

    sent = call(
        functools.partial(pack_body, cap),
        shape((n_z, SLOT_ROWS, part), BF16),
        [SMEM, SMEM, VMEM],
        [pltpu.VMEM(((EXPERTS + 1) * SLOT_ROWS, part), F32)],
        moved=500_000,
        mib=56,
    )(routes_t, probs_t, d_out)
    first = lax.all_to_all(sent, "z", split_axis=0, concat_axis=0, tiled=True)

    x_own, x_other, act, slope, hidden = call(
        functools.partial(early_body, cap, n_x, block, own),
        (
            shape((half, rows), BF16),
            shape((half, rows), BF16),
            shape((rows, hid), F32),
            shape((rows, hid), F32),
            shape((rows, hid), BF16),
        ),
        [SMEM, HBM, HBM, HBM],
        [
            pltpu.VMEM((rows, width), BF16),
            pltpu.VMEM((width, rows), BF16),
            pltpu.VMEM(x_in.shape, BF16),
            pltpu.VMEM(w_gate.shape, BF16),
            pltpu.VMEM(w_up.shape, BF16),
            pltpu.VMEM((half, rows), BF16),
            pltpu.VMEM((half, rows), BF16),
            pltpu.VMEM((rows, hid), F32),
            pltpu.VMEM((rows, hid), F32),
            pltpu.VMEM((rows, hid), BF16),
            pltpu.SemaphoreType.DMA((8,)),
        ],
        mib=60,
        out_specs=(HBM,) * 5,
        flops=2 * rows * width * (2 * hid + 2 * rows),
        moved=2 * width * (2 * hid + 2 * rows) + 10 * rows * hid,
    )(where, x_in, w_gate, w_up)

    def swap(v):
        return lax.ppermute(v, "c", [(i, (i + 1) % n_c) for i in range(n_c)])

    def shift(v, by):
        return lax.ppermute(v, "x", [(i, (i + by) % n_x) for i in range(n_x)])

    x_pair = swap(x_other)
    hidden_pair = swap(hidden)

    first, x_pair, hidden_pair = lax.optimization_barrier((first, x_pair, hidden_pair))
    mine = first.reshape(packed, part)
    bufs = [mine] + [shift(mine, -j) for j in range(1, n_x)]
    bufs[1], act, slope = lax.optimization_barrier((bufs[1], act, slope))
    act, slope = call(
        hold_body,
        (shape((rows, hid), F32), shape((rows, hid), F32)),
        [HBM] * 2,
        [pltpu.SemaphoreType.DMA((2,))],
        moved=16 * rows * hid,
    )(act, slope)
    ship, y_own = call(
        functools.partial(middle_body, cap, block, used, own),
        (shape((half + 2 * hid, rows), BF16), shape((half, rows), BF16)),
        [SMEM] + [VMEM] * (n_x + 3),
        [pltpu.VMEM((rows, width), BF16), pltpu.VMEM((width, rows), BF16)],
        flops=2 * rows * width * (hid + rows),
        moved=2 * width * (hid + 2 * rows) + 10 * rows * hid,
    )(where, *bufs, w_down, act, slope)
    got = swap(ship)

    back = call(
        functools.partial(back_body, block, half),
        tuple(shape((block, width), BF16) for _ in range(n_x)),
        [VMEM] * 3,
        flops=2 * rows * width * 2 * hid,
        moved=2 * width * (2 * hid + rows),
    )(ship, w_gate, w_up)
    got, back = lax.optimization_barrier((got, back))

    steps = n_y // 2
    terms = call(
        functools.partial(terms_body, own, hid, steps),
        shape((n_y, 3, own, hid), BF16),
        [VMEM] * 7,
        [pltpu.VMEM((n_y, 3, own, hid), BF16), pltpu.SemaphoreType.DMA((steps,))],
        flops=2 * 2 * rows * half * 3 * hid,
        moved=2 * half * (3 * hid + 4 * rows),
        mib=24,
        out_specs=HBM,
    )(x_own, x_pair, y_own, ship, got, hidden, hidden_pair)
    shares = lax.psum_scatter(
        terms.reshape(n_y * 3 * own, hid), "y", scatter_dimension=0, tiled=True
    )
    weight_grads = shares.reshape(3, own, hid)

    arrived = [back[0]] + [shift(back[j], j) for j in range(1, n_x)]
    added = call(
        functools.partial(merge_body, cap, used),
        shape((n_z, SLOT_ROWS, part), BF16),
        [VMEM] * n_x,
        [pltpu.VMEM((packed, part), BF16)],
        flops=2 * packed * block * width,
        moved=2 * n_x * block * width,
    )(*arrived)
    returned = lax.all_to_all(
        added, "z", split_axis=0, concat_axis=0, tiled=True
    )
    input_grad = call(
        functools.partial(final_body, cap),
        shape((tokens, width), BF16),
        [SMEM, VMEM],
        [pltpu.VMEM(((EXPERTS + 1) * SLOT_ROWS, part), F32), pltpu.VMEM((16, width), F32)],
        moved=500_000,
    )(routes_t, returned)
    return (input_grad, weight_grads)


def solution(mesh):
    n_z = mesh.shape["expert"] // 4
    fine = Mesh(
        mesh.devices.reshape(mesh.shape["dp"] // 2, 2, n_z, 4), ("y", "c", "z", "x")
    )
    dp, expert = ("y", "c"), ("z", "x")
    every = dp + expert
    return jax.shard_map(
        per_device,
        mesh=fine,
        in_specs=(
            P(every, None),
            P(every, None),
            P(every, None),
            P(dp, expert, None, None),
            P(expert, None),
            P(expert, None),
            P(expert, None),
        ),
        out_specs=(P(every, None), P(None, dp, expert)),
        check_vma=False,
    )
```

```python
import functools

import jax
import jax.numpy as jnp
from jax import lax
from jax.experimental import pallas as pl
from jax.experimental.pallas import tpu as pltpu
from jax.sharding import Mesh, PartitionSpec as P

EXPERTS = 2
SLOT_ROWS = 16
PARTS = 3
TILE = 256
F32 = jnp.float32
BF16 = jnp.bfloat16
MIB = 1024 * 1024
NT = (((1,), (1,)), ((), ()))
TN = (((0,), (0,)), ((), ()))
VMEM = pl.BlockSpec(memory_space=pltpu.VMEM)
SMEM = pl.BlockSpec(memory_space=pltpu.SMEM)
HBM = pl.BlockSpec(memory_space=pltpu.HBM)


def call(body, out_shape, in_specs, scratch=(), flops=0, moved=0, mib=16, **more):
    return pl.pallas_call(
        body,
        out_shape=out_shape,
        in_specs=in_specs,
        scratch_shapes=list(scratch),
        compiler_params=pltpu.CompilerParams(vmem_limit_bytes=mib * MIB),
        cost_estimate=pl.CostEstimate(flops=flops, bytes_accessed=moved, transcendentals=0),
        **more,
    )


def walk(routes_ref, tokens):
    counts = [jnp.int32(0)] * EXPERTS
    for token in range(tokens):
        for choice in range(2):
            expert = routes_ref[choice, token]
            row = jnp.int32(EXPERTS * SLOT_ROWS)
            for e in range(EXPERTS):
                here = expert == e
                row = jnp.where(here, e * SLOT_ROWS + counts[e], row)
                counts[e] = counts[e] + here.astype(jnp.int32)
            yield token, choice, row


def pack_body(cap, routes_ref, probs_ref, d_ref, out_ref, rows):
    tokens, width = d_ref.shape
    part = width // PARTS
    rows[...] = jnp.zeros_like(rows)
    d = d_ref[...].astype(F32)
    for token, choice, row in walk(routes_ref, tokens):
        scaled = probs_ref[choice, token] * d[token : token + 1, :]
        for p in range(PARTS):
            rows[pl.ds(row + p * cap, 1), :] = scaled[:, p * part : (p + 1) * part]
    depth = out_ref.shape[0] // EXPERTS
    for e in range(EXPERTS):
        block = rows[e * SLOT_ROWS : (e + 1) * SLOT_ROWS, :].astype(BF16)
        for k in range(depth):
            out_ref[e * depth + k] = block


def eye():
    i = lax.broadcasted_iota(jnp.int32, (TILE, TILE), 0)
    j = lax.broadcasted_iota(jnp.int32, (TILE, TILE), 1)
    return (i == j).astype(BF16)


def split_halves(full, core, own_ref, other_ref, own):
    groups = full.shape[0] // (2 * own)
    for g in range(groups):
        mine = pl.multiple_of(g * 2 * own + core * own, 16)
        theirs = pl.multiple_of(g * 2 * own + (1 - core) * own, 16)
        own_ref[g * own : (g + 1) * own, :] = full[pl.ds(mine, own), :]
        other_ref[g * own : (g + 1) * own, :] = full[pl.ds(theirs, own), :]


def start_all(pairs, sems, first=0):
    copies = [pltpu.make_async_copy(a, b, sems.at[first + n]) for n, (a, b) in enumerate(pairs)]
    for copy in copies:
        copy.start()
    return copies


def early_body(cap, n_x, block, own, where_ref, x_at, wg_at, wu_at, own_at, other_at, act_at, slope_at, hidden_at, *scratch):
    xp, xt, x_ref, wg_ref, wu_ref, own_ref, other_ref, act_ref, slope_ref, hidden_ref, sems = scratch
    fetches = start_all(((x_at, x_ref), (wg_at, wg_ref), (wu_at, wu_ref)), sems)
    rows, width = xp.shape
    used = x_ref.shape[0] // n_x
    at = where_ref[0]
    core = where_ref[1]
    r = lax.broadcasted_iota(jnp.int32, (rows, x_ref.shape[0]), 0)
    q = lax.broadcasted_iota(jnp.int32, (rows, x_ref.shape[0]), 1)
    i = r % block
    source = (at + r // block) % n_x
    order = ((q == ((i // cap) * n_x + source) * cap + i % cap) & (i < used)).astype(BF16)
    one = eye()
    fetches[0].wait()
    for t in range(width // TILE):
        piece = jnp.dot(order, x_ref[:, t * TILE : (t + 1) * TILE], preferred_element_type=F32).astype(BF16)
        xp[:, t * TILE : (t + 1) * TILE] = piece
        xt[t * TILE : (t + 1) * TILE, :] = lax.dot_general(one, piece, NT, preferred_element_type=F32).astype(BF16)
    split_halves(xt, core, own_ref, other_ref, own)
    stores = start_all(((other_ref, other_at), (own_ref, own_at)), sems, 3)
    fetches[1].wait()
    gate = lax.dot_general(xp[...], wg_ref[...], NT, preferred_element_type=F32)
    fetches[2].wait()
    upper = lax.dot_general(xp[...], wu_ref[...], NT, preferred_element_type=F32)
    sigma = jax.nn.sigmoid(gate)
    act = gate * sigma
    act_ref[...] = act
    slope_ref[...] = upper * sigma * (1.0 + gate * (1.0 - sigma))
    hidden_ref[...] = (act * upper).astype(BF16)
    stores += start_all(((hidden_ref, hidden_at), (act_ref, act_at), (slope_ref, slope_at)), sems, 5)
    for store in stores:
        store.wait()


def hold_body(act_at, slope_at, act_ref, slope_ref, sems):
    for copy in start_all(((act_at, act_ref), (slope_at, slope_ref)), sems):
        copy.wait()


def picker(cap, block, used, packed, part):
    i = lax.broadcasted_iota(jnp.int32, (block, packed), 0)
    q = lax.broadcasted_iota(jnp.int32, (block, packed), 1)
    return ((q == (i // cap) * SLOT_ROWS + part * cap + i % cap) & (i < used)).astype(BF16)


def middle_body(cap, block, used, own, where_ref, *refs):
    *bufs, wd_ref, act_ref, slope_ref, ship_ref, own_ref, dy, dyt = refs
    core = where_ref[1]
    packed, part = bufs[0].shape
    hid, width = wd_ref.shape
    half = width // 2
    rows = dy.shape[0]
    for p in range(PARTS):
        pick = picker(cap, block, used, packed, p)
        for j, buf in enumerate(bufs):
            dy[j * block : (j + 1) * block, p * part : (p + 1) * part] = jnp.dot(
                pick, buf[...], preferred_element_type=F32
            ).astype(BF16)
    d_hidden = lax.dot_general(dy[...], wd_ref[...], NT, preferred_element_type=F32)
    both = jnp.concatenate([d_hidden * slope_ref[...], d_hidden * act_ref[...]], axis=1).astype(BF16)
    for k in range(2 * hid // rows):
        ship_ref[half + k * rows : half + (k + 1) * rows, :] = both[:, k * rows : (k + 1) * rows]
    one = eye()
    for t in range(width // TILE):
        dyt[t * TILE : (t + 1) * TILE, :] = lax.dot_general(
            one, dy[:, t * TILE : (t + 1) * TILE], NT, preferred_element_type=F32
        ).astype(BF16)
    split_halves(dyt, core, own_ref, ship_ref, own)


def columns(ref, first, rows, n):
    return [ref[first + k * rows : first + (k + 1) * rows, :] for k in range(n // rows)]


def back_body(block, first, ship_ref, wg_ref, wu_ref, *outs):
    hid, width = wg_ref.shape
    step = 2 * TILE
    both = jnp.concatenate(columns(ship_ref, first, ship_ref.shape[1], 2 * hid), axis=1)
    for t in range(width // step):
        cols = slice(t * step, (t + 1) * step)
        dx = jnp.dot(both[:, :hid], wg_ref[:, cols], preferred_element_type=F32)
        dx = (dx + jnp.dot(both[:, hid:], wu_ref[:, cols], preferred_element_type=F32)).astype(BF16)
        for j, out in enumerate(outs):
            out[:, cols] = dx[j * block : (j + 1) * block, :]


def merge_body(cap, used, *refs):
    *bufs, out_ref, pack = refs
    block, width = bufs[0].shape
    depth = out_ref.shape[0]
    part = width // PARTS
    packed = depth * SLOT_ROWS
    i = lax.broadcasted_iota(jnp.int32, (packed, block), 1)
    q = lax.broadcasted_iota(jnp.int32, (packed, block), 0)
    for h in range(part // TILE):
        total = None
        for p in range(PARTS):
            cols = slice(p * part + h * TILE, p * part + (h + 1) * TILE)
            added = bufs[0][:, cols].astype(F32)
            for buf in bufs[1:]:
                added = added + buf[:, cols].astype(F32)
            put = ((q == (i // cap) * SLOT_ROWS + p * cap + i % cap) & (i < used)).astype(BF16)
            term = jnp.dot(put, added.astype(BF16), preferred_element_type=F32)
            total = term if total is None else total + term
        pack[:, h * TILE : (h + 1) * TILE] = total.astype(BF16)
    for k in range(depth):
        out_ref[k] = pack[k * SLOT_ROWS : (k + 1) * SLOT_ROWS, :]


def terms_body(own, hid, steps, xo, xp, yo, ship, got, ho, hp, out_at, stage, sems):
    half, rows = xo.shape
    per = out_at.shape[0] // steps
    depth = per * own
    d_own = jnp.concatenate(columns(ship, half, rows, 2 * hid), axis=1)
    d_pair = jnp.concatenate(columns(got, half, rows, 2 * hid), axis=1)
    stores = []
    for s in range(steps):
        here = slice(s * depth, (s + 1) * depth)
        both = jnp.dot(xo[here, :], d_own, preferred_element_type=F32)
        both = (both + jnp.dot(xp[here, :], d_pair, preferred_element_type=F32)).astype(BF16)
        down = jnp.dot(yo[here, :], ho[...], preferred_element_type=F32)
        down = (down + jnp.dot(got[here, :], hp[...], preferred_element_type=F32)).astype(BF16)
        for g in range(per):
            part = slice(g * own, (g + 1) * own)
            stage[s * per + g, 0] = both[part, :hid]
            stage[s * per + g, 1] = both[part, hid:]
            stage[s * per + g, 2] = down[part, :]
        groups = pl.ds(s * per, per)
        stores += start_all(((stage.at[groups], out_at.at[groups]),), sems, s)
    for store in stores:
        store.wait()


def final_body(cap, routes_ref, back_ref, out_ref, sums, grads):
    depth = back_ref.shape[0] // EXPERTS
    tokens, width = out_ref.shape
    part = width // PARTS
    for e in range(EXPERTS):
        total = back_ref[e * depth].astype(F32)
        for k in range(1, depth):
            total = total + back_ref[e * depth + k].astype(F32)
        sums[e * SLOT_ROWS : (e + 1) * SLOT_ROWS, :] = total
    sums[EXPERTS * SLOT_ROWS :, :] = jnp.zeros((SLOT_ROWS, part), F32)
    held = [None, None]
    for token, choice, row in walk(routes_ref, tokens):
        held[choice] = row
        if choice == 1:
            for p in range(PARTS):
                grads[token : token + 1, p * part : (p + 1) * part] = (
                    sums[pl.ds(held[0] + p * cap, 1), :] + sums[pl.ds(held[1] + p * cap, 1), :]
                )
    out_ref[...] = grads[:tokens, :].astype(BF16)


def per_device(d_out, routes, probs, saved_inputs, w_gate, w_up, w_down):
    n_y, n_c, n_z, n_x = (lax.axis_size(a) for a in ("y", "c", "z", "x"))
    tokens, width = d_out.shape
    cap = tokens // 2
    hid = w_gate.shape[0]
    part = width // PARTS
    used = n_z * cap
    block = -(-used // 16) * 16
    rows = n_x * block
    packed = n_z * SLOT_ROWS
    own = width // (n_y * n_c)
    half = width // 2
    routes_t = routes.T
    probs_t = probs.T
    where = jnp.stack([lax.axis_index("x"), lax.axis_index("c")]).astype(jnp.int32)
    shape = jax.ShapeDtypeStruct
    x_in = saved_inputs.reshape(n_z * n_x * cap, width)

    sent = call(
        functools.partial(pack_body, cap),
        shape((n_z, SLOT_ROWS, part), BF16),
        [SMEM, SMEM, VMEM],
        [pltpu.VMEM(((EXPERTS + 1) * SLOT_ROWS, part), F32)],
        moved=500_000,
        mib=56,
    )(routes_t, probs_t, d_out)
    first = lax.all_to_all(sent, "z", split_axis=0, concat_axis=0, tiled=True)

    x_own, x_other, act, slope, hidden = call(
        functools.partial(early_body, cap, n_x, block, own),
        (
            shape((half, rows), BF16),
            shape((half, rows), BF16),
            shape((rows, hid), F32),
            shape((rows, hid), F32),
            shape((rows, hid), BF16),
        ),
        [SMEM, HBM, HBM, HBM],
        [
            pltpu.VMEM((rows, width), BF16),
            pltpu.VMEM((width, rows), BF16),
            pltpu.VMEM(x_in.shape, BF16),
            pltpu.VMEM(w_gate.shape, BF16),
            pltpu.VMEM(w_up.shape, BF16),
            pltpu.VMEM((half, rows), BF16),
            pltpu.VMEM((half, rows), BF16),
            pltpu.VMEM((rows, hid), F32),
            pltpu.VMEM((rows, hid), F32),
            pltpu.VMEM((rows, hid), BF16),
            pltpu.SemaphoreType.DMA((8,)),
        ],
        mib=60,
        out_specs=(HBM,) * 5,
        flops=2 * rows * width * (2 * hid + 2 * rows),
        moved=2 * width * (2 * hid + 2 * rows) + 10 * rows * hid,
    )(where, x_in, w_gate, w_up)

    def swap(v):
        return lax.ppermute(v, "c", [(i, (i + 1) % n_c) for i in range(n_c)])

    def shift(v, by):
        return lax.ppermute(v, "x", [(i, (i + by) % n_x) for i in range(n_x)])

    nearest = sorted(range(1, n_x), key=lambda j: min(j, n_x - j))

    x_pair = swap(x_other)
    hidden_pair = swap(hidden)

    first, x_pair, hidden_pair = lax.optimization_barrier((first, x_pair, hidden_pair))
    mine = first.reshape(packed, part)
    moved = {j: shift(mine, -j) for j in nearest}
    bufs = [mine] + [moved[j] for j in range(1, n_x)]
    bufs[1], act, slope = lax.optimization_barrier((bufs[1], act, slope))
    act, slope = call(
        hold_body,
        (shape((rows, hid), F32), shape((rows, hid), F32)),
        [HBM] * 2,
        [pltpu.SemaphoreType.DMA((2,))],
        moved=16 * rows * hid,
    )(act, slope)
    ship, y_own = call(
        functools.partial(middle_body, cap, block, used, own),
        (shape((half + 2 * hid, rows), BF16), shape((half, rows), BF16)),
        [SMEM] + [VMEM] * (n_x + 3),
        [pltpu.VMEM((rows, width), BF16), pltpu.VMEM((width, rows), BF16)],
        flops=2 * rows * width * (hid + rows),
        moved=2 * width * (hid + 2 * rows) + 10 * rows * hid,
    )(where, *bufs, w_down, act, slope)
    got = swap(ship)

    back = call(
        functools.partial(back_body, block, half),
        tuple(shape((block, width), BF16) for _ in range(n_x)),
        [VMEM] * 3,
        flops=2 * rows * width * 2 * hid,
        moved=2 * width * (2 * hid + rows),
    )(ship, w_gate, w_up)
    got, back = lax.optimization_barrier((got, back))

    steps = n_y // 2
    terms = call(
        functools.partial(terms_body, own, hid, steps),
        shape((n_y, 3, own, hid), BF16),
        [VMEM] * 7,
        [pltpu.VMEM((n_y, 3, own, hid), BF16), pltpu.SemaphoreType.DMA((steps,))],
        flops=2 * 2 * rows * half * 3 * hid,
        moved=2 * half * (3 * hid + 4 * rows),
        mib=24,
        out_specs=HBM,
    )(x_own, x_pair, y_own, ship, got, hidden, hidden_pair)
    shares = lax.psum_scatter(
        terms.reshape(n_y * 3 * own, hid), "y", scatter_dimension=0, tiled=True
    )
    weight_grads = shares.reshape(3, own, hid)

    arrived = [back[0]] + [shift(back[j], j) for j in nearest]
    added = call(
        functools.partial(merge_body, cap, used),
        shape((n_z, SLOT_ROWS, part), BF16),
        [VMEM] * n_x,
        [pltpu.VMEM((packed, part), BF16)],
        flops=2 * packed * block * width,
        moved=2 * n_x * block * width,
    )(*arrived)
    returned = lax.all_to_all(
        added, "z", split_axis=0, concat_axis=0, tiled=True
    )
    input_grad = call(
        functools.partial(final_body, cap),
        shape((tokens, width), BF16),
        [SMEM, VMEM],
        [pltpu.VMEM(((EXPERTS + 1) * SLOT_ROWS, part), F32), pltpu.VMEM((16, width), F32)],
        moved=500_000,
    )(routes_t, returned)
    return (input_grad, weight_grads)


def solution(mesh):
    n_z = mesh.shape["expert"] // 4
    fine = Mesh(
        mesh.devices.reshape(mesh.shape["dp"] // 2, 2, n_z, 4), ("y", "c", "z", "x")
    )
    dp, expert = ("y", "c"), ("z", "x")
    every = dp + expert
    return jax.shard_map(
        per_device,
        mesh=fine,
        in_specs=(
            P(every, None),
            P(every, None),
            P(every, None),
            P(dp, expert, None, None),
            P(expert, None),
            P(expert, None),
            P(expert, None),
        ),
        out_specs=(P(every, None), P(None, dp, expert)),
        check_vma=False,
    )
```
